32 devices in a mesh: row: 4 (over y, x), col: 8 (over z, core).
Axes of the slice: x: 2, y: 2, z: 4, core: 2. Of those that a mesh axis runs over, the one named last changes fastest.
Arguments:
- values: bfloat16 [4096, 4096], P('row', 'col'), may hold values from -1.5 to 1.5
- pattern: int32 [16, 16], P('row', 'col'), may hold values from 0 to 1, as said below
- sections: int32 [4], replicated, may hold values from 0 to 15
Outputs:
- exposure: bfloat16 [4096, 4096], P('row', 'col')
The draws below stay inside these ranges and needn't reach their ends.
Inputs may be any that keep to these rules, and one draw needn't show every extreme that they name: `pattern`: 1 where a tile is stored, else 0; the share of stored tiles differs from tile row to tile row.
All inputs are finite; a program needn't handle non-finite values.
Results may differ from the reference program's by a relative error of at most 0.001.
Values may be sent and summed in bfloat16 or wider, within the bound.
No kernel may reach another device: no remote copies, remote signals or barrier semaphores. Data moves between devices by JAX's collectives and lax.ppermute only.
A program may use at most 64 MiB of HBM per device.

```python
import jax
import jax.numpy as jnp
from jax import lax

TILE = 256
SECTIONS = 4
NT = 16
N = 4096


def draw_pattern(key, part):
    key = jax.random.fold_in(key, 7)
    level_key, roll_key = jax.random.split(key)
    levels = jax.random.randint(level_key, (NT, 1), 0, 4)
    rolls = jax.random.randint(roll_key, (NT, NT), 0, 8)
    return (rolls < 2 + 2 * levels).astype(jnp.int32)


def plant(array, own_key, smallest, high):
    shape = array.shape
    place = [jax.random.randint(jax.random.fold_in(own_key, axis), (), 0, shape[axis]) for axis in range(len(shape))]
    array = array.at[tuple(place)].set(smallest)
    longest = shape.index(max(shape))
    place[longest] = (place[longest] + 1) % shape[longest]
    return array.at[tuple(place)].set(high)


def block_levels(stream_key, dims, cuts, low, largest):
    gain = 1.0
    for position, shards_of in cuts:
        heights = jax.random.uniform(jax.random.fold_in(jax.random.fold_in(stream_key, 6), position), (shards_of,), jnp.float32, low / len(cuts), largest / len(cuts))
        gain = gain * jnp.repeat(jnp.exp(heights), dims[position] // shards_of).reshape((-1,) + (1,) * (len(dims) - 1 - position))
    return gain


def noise(own_key, shape, scale, bound, cuts=(), kind=jnp.bfloat16):
    drawn = jax.random.normal(own_key, shape, jnp.float32) * scale
    if len(cuts) > 0:
        drawn = block_levels(own_key, shape, cuts, -0.22, 0.18) * drawn
    return jnp.clip(drawn, min=-bound, max=bound).astype(kind)


def setup_inputs(seed: int = 0) -> dict:
    streams_of = jax.random.split(jax.random.key(seed), 4)
    return {
        "values": noise(streams_of[0], (N, N), 0.25, 1.5, ((0, 4), (1, 8))),
        "pattern": draw_pattern(jax.random.fold_in(streams_of[3], 71), 0),
        "sections": plant(jax.random.randint(streams_of[2], (SECTIONS,), 0, NT), jax.random.fold_in(streams_of[2], 1), 0, NT - 1).astype(jnp.int32),
    }


def reference(values, pattern, sections):
    flags = pattern.astype(jnp.bfloat16)
    column_list = []
    row_list = []
    for section_number in range(SECTIONS):
        section_index = sections[section_number].astype(jnp.int32)
        column_piece = lax.dynamic_slice_in_dim(values, section_index * TILE, TILE, 1)
        column_flags = lax.dynamic_slice_in_dim(flags, section_index, 1, 1)
        column_piece = column_piece * jnp.repeat(column_flags, TILE, axis=0)
        row_piece = lax.dynamic_slice_in_dim(values, section_index * TILE, TILE, 0)
        row_flags = lax.dynamic_slice_in_dim(flags, section_index, 1, 0)
        row_piece = row_piece * jnp.repeat(row_flags, TILE, axis=1)
        column_list.append(column_piece)
        row_list.append(row_piece)
    left_panels = jnp.concatenate(column_list, axis=1)
    right_panels = jnp.concatenate(row_list, axis=0)

    def tile_row_product(tile_row):
        left_rows = lax.dynamic_slice_in_dim(left_panels, tile_row * TILE, TILE, 0)
        return jnp.dot(left_rows, right_panels, preferred_element_type=jnp.float32).astype(jnp.bfloat16)

    blocks = lax.map(tile_row_product, jnp.arange(NT, dtype=jnp.int32))
    return blocks.reshape(N, N)
```

```python
import functools

import jax
import jax.numpy as jnp
from jax import lax
from jax.experimental import pallas as pl
from jax.experimental.pallas import tpu as pltpu
from jax.sharding import PartitionSpec as P

TILE = 256
SECTIONS = 4
CORES = 2
PARTS = 2
LAG = 2
PAIR = 2
STRIP = 128
BF16 = jnp.bfloat16
ANY = pl.BlockSpec(memory_space=pl.ANY)
SMEM = pl.BlockSpec(memory_space=pltpu.SMEM)
VMEM = pl.BlockSpec(memory_space=pltpu.VMEM)
HBM = pl.BlockSpec(memory_space=pltpu.HBM)
PARAMS = pltpu.CompilerParams(vmem_limit_bytes=32 * 1024 * 1024)


def quotient(x, n):
    return lax.shift_right_logical(x, jnp.int32(n.bit_length() - 1)) if n & (n - 1) == 0 else lax.div(x, jnp.int32(n))


def remainder(x, n):
    return x & (n - 1) if n & (n - 1) == 0 else lax.rem(x, jnp.int32(n))


def slots(owners, chips):
    flows = [o < chips - 1 for o in owners]

    def ahead(i, s):
        return flows[i] & ((owners[i] >= owners[s]) if i < s else (owners[i] > owners[s]))

    ranks = [
        sum(ahead(i, s).astype(jnp.int32) for i in range(SECTIONS) if i != s) for s in range(SECTIONS)
    ]
    firsts = []
    steps = jnp.int32(0)
    for s in range(SECTIONS):
        first = -LAG * owners[s]
        for j in range(SECTIONS):
            if j != s:
                pushed = (ranks[s] - ranks[j]) * PARTS - LAG * owners[j]
                first = jnp.where(ahead(j, s), jnp.maximum(first, pushed), first)
        firsts.append(first)
        steps = jnp.where(flows[s], jnp.maximum(steps, first + PARTS + LAG * (chips - 2)), steps)
    return firsts, steps


def owners_of(sections, col_tiles):
    return [quotient(sections[s], col_tiles * CORES) for s in range(SECTIONS)]


def lines(sections, col_tiles, chips):
    owners = owners_of(sections, col_tiles)
    return owners, [chips - 1 - o for o in owners]


def most_steps(chips):
    return SECTIONS * PARTS + LAG * (chips - 2)


def size_keys(rows, chips):
    most = most_steps(chips)
    if rows != 4 or chips > 4:
        return [(most, SECTIONS, SECTIONS)]
    return [
        (most - (SECTIONS - count) * PARTS, PAIR if count <= PAIR else SECTIONS, min(count + 1, SECTIONS))
        for count in range(1, SECTIONS + 1)
    ]


def largest(values):
    return functools.reduce(jnp.maximum, values)


def prepare_kernel(rows, col_tiles, row_tiles, chips, sections_in, pattern_in, values, *refs):
    masked = refs[:PARTS]
    table, which, again, sections, pattern, sems, small = refs[PARTS:]
    height = row_tiles * TILE // PARTS
    col = lax.axis_index("col")
    chip, core = quotient(col, CORES), remainder(col, CORES)
    most = most_steps(chips)

    def fetch(r, c):
        block = values.at[pl.ds(r * TILE, TILE), pl.ds(c * TILE, TILE)]
        part, start = r * TILE // height, r * TILE % height
        return pltpu.make_async_copy(block, masked[part].at[c, start : start + TILE, :], sems.at[c, r])

    lists = [
        pltpu.make_async_copy(sections_in, sections, small.at[0]),
        pltpu.make_async_copy(pattern_in, pattern, small.at[1]),
    ]
    for copy in lists:
        copy.start()
    for r in range(row_tiles):
        for c in range(col_tiles):
            fetch(r, c).start()
    table[...] = jnp.full(table.shape, -1, jnp.int32)

    def note(row, item):
        table[pl.ds(row, 1), :] = jnp.full((1, table.shape[1]), item, jnp.int32)

    for copy in lists:
        copy.wait()
    up, down = lines(sections, col_tiles, chips)
    needed = jnp.int32(0)
    for flow, line in enumerate((up, down)):
        place = chip if flow == 0 else chips - 1 - chip
        firsts, steps = slots(line, chips)
        needed = jnp.maximum(needed, steps)
        mine = core == flow
        for s in range(SECTIONS):

            @pl.when(mine & (line[s] == place) & (line[s] < chips - 1))
            def _():
                local = sections[s] - up[s] * (col_tiles * CORES)
                for part in range(PARTS):
                    note(firsts[s] + LAG * place + part, local)

            @pl.when(line[s] < place)
            def _():
                for part in range(PARTS):
                    note(jnp.where(mine, most, 2 * most) + firsts[s] + LAG * (place - 1) + part, s)

    for s in range(SECTIONS):

        @pl.when(up[s] == chip)
        def _():
            note(3 * most + s, sections[s] - up[s] * (col_tiles * CORES))

    if rows == 4:
        note_rows(note, 3 * most + SECTIONS, sections, row_tiles, core)
    keys = size_keys(rows, chips)
    number = jnp.int32(0)
    if len(keys) > 1:
        owners = [quotient(sections[s], row_tiles) for s in range(SECTIONS)]
        counts = [sum((o == r).astype(jnp.int32) for o in owners) for r in range(4)]
        in_row = largest(counts)
        in_pair = largest([counts[i] + counts[j] for i, j in ((0, 1), (2, 3), (0, 2), (1, 3))])
        for key in keys[:-1]:
            fits = (needed <= key[0]) & (in_row <= key[1]) & (in_pair <= key[2])
            number = number + jnp.where(fits, 0, 1)
    which[0] = number
    for s in range(SECTIONS):
        again[s] = sections[s]

    for r in range(row_tiles):
        for c in range(col_tiles):
            fetch(r, c).wait()
            part, start = r * TILE // height, r * TILE % height

            @pl.when(pattern[c, r] == 0)
            def _():
                masked[part][c, start : start + TILE, :] = jnp.zeros((TILE, TILE), BF16)


def rank_among(owners, s):
    return sum((owners[i] == owners[s]).astype(jnp.int32) for i in range(s)) + jnp.int32(0)


def bits(owner, first):
    x, y = remainder(owner, 2), quotient(owner, 2)
    return jnp.where(first, x, y), jnp.where(first, y, x)


def note_rows(note, start, sections, row_tiles, core):
    row = lax.axis_index("row")
    first = core == 0
    here = bits(row, first)
    owners = [quotient(sections[s], row_tiles) for s in range(SECTIONS)]
    pairs = [bits(o, first)[1] for o in owners]
    for s in range(SECTIONS):
        rank, slot = rank_among(owners, s), rank_among(pairs, s)

        @pl.when(owners[s] == row)
        def _():
            note(start + rank, sections[s] - owners[s] * row_tiles)

        @pl.when(pairs[s] == here[1])
        def _():
            note(start + SECTIONS + slot, rank + jnp.where(bits(owners[s], first)[0] == here[0], 0, SECTIONS))

        note(start + 2 * SECTIONS + s, slot + jnp.where(pairs[s] == here[1], 0, SECTIONS))


def own_rows_kernel(col_tiles, row_tiles, start, table, *refs):
    masked, outs = refs[:PARTS], refs[PARTS:]
    in_part = row_tiles // PARTS
    places = [(out, place) for out in outs for place in range(PAIR)]
    tiles = [jnp.max(table[start + i : start + i + 1, :]) for i in range(len(places))]
    for (out, place), tile in zip(places, tiles):
        local = jnp.maximum(tile, 0)
        for part in range(PARTS):
            first = pl.multiple_of((local - part * in_part) * TILE, TILE)

            @pl.when((tile >= 0) & (quotient(local, in_part) == part))
            def _():
                for c in range(col_tiles):
                    out[place, :, c * TILE : (c + 1) * TILE] = masked[part][c, pl.ds(first, TILE), :]


def masked_rows_kernel(col_tiles, row_tiles, sections, *refs):
    masked, out = refs[:PARTS], refs[-1]
    row = lax.axis_index("row")
    in_part = row_tiles // PARTS
    for s in range(SECTIONS):
        owner = quotient(sections[s], row_tiles)
        local = sections[s] - owner * row_tiles
        out[s] = jnp.zeros(out.shape[1:], BF16)
        for part in range(PARTS):
            first = pl.multiple_of((local - part * in_part) * TILE, TILE)

            @pl.when((owner == row) & (quotient(local, in_part) == part))
            def _():
                for c in range(col_tiles):
                    out[s, :, c * TILE : (c + 1) * TILE] = masked[part][c, pl.ds(first, TILE), :]


def near_rows_kernel(start, table, *refs):
    out = refs[-1]
    arrays = len(refs) // 2 - 1
    own, got = refs[:arrays], refs[arrays : 2 * arrays]
    sources = [jnp.max(table[start + i : start + i + 1, :]) for i in range(out.shape[0])]
    for i, source in enumerate(sources):
        rank = remainder(jnp.maximum(source, 0), SECTIONS)
        place = remainder(rank, PAIR)
        for number in range(arrays):
            wanted = (source >= 0) & (quotient(rank, PAIR) == number)

            @pl.when(wanted & (source < SECTIONS))
            def _():
                out[i] = own[number][place]

            @pl.when(wanted & (source >= SECTIONS))
            def _():
                out[i] = got[number][place]


def all_rows_kernel(start, table, near, far, out):
    sources = [jnp.max(table[start + s : start + s + 1, :]) for s in range(SECTIONS)]
    for s, source in enumerate(sources):
        slot = remainder(source, SECTIONS)

        @pl.when(source < SECTIONS)
        def _():
            out[s] = near[slot]

        @pl.when(source >= SECTIONS)
        def _():
            out[s] = far[slot]


def choose_kernel(col_tiles, t, table, masked, got, *refs):
    out = refs[-1]
    core = remainder(lax.axis_index("col"), CORES)
    tile = jnp.max(table[t : t + 1, :])
    local, owner = remainder(jnp.maximum(tile, 0), col_tiles), quotient(jnp.maximum(tile, 0), col_tiles)

    def copy_from(ref, *index):
        @pl.loop(0, out.shape[0] // STRIP)
        def _(i):
            strip = pl.ds(pl.multiple_of(i * STRIP, STRIP), STRIP)
            out[strip, :] = ref[(*index, strip, slice(None))]

    @pl.when((tile >= 0) & (owner == core))
    def _():
        copy_from(masked, local)

    @pl.when((tile >= 0) & (owner != core))
    def _():
        copy_from(got, local)

    if t >= LAG:

        @pl.when(tile < 0)
        def _():
            copy_from(refs[0])


def panel_columns(s):
    return pl.ds(pl.multiple_of(s * TILE, TILE), TILE)


def arrivals(table, most, times, direct, passed):
    rows = [(entry * most + t, source) for t, d, p in zip(times, direct, passed) for entry, source in ((1, d), (2, p))]
    return [(jnp.max(table[row : row + 1, :]), source) for row, source in rows]


def gather_panel(col_tiles, most, times, table, masked, got, direct, passed, left, sem):
    core = remainder(lax.axis_index("col"), CORES)
    copies = []
    for s in range(SECTIONS):
        row = 3 * most + s
        tile = jnp.max(table[row : row + 1, :])
        local, owner = remainder(jnp.maximum(tile, 0), col_tiles), quotient(jnp.maximum(tile, 0), col_tiles)
        target = left.at[:, s * TILE : (s + 1) * TILE]
        copies.append(((tile >= 0) & (owner == core), masked.at[local], target))
        copies.append(((tile >= 0) & (owner != core), got.at[local], target))
    for s, source in arrivals(table, most, times, direct, passed):
        copies.append((s >= 0, source, left.at[:, panel_columns(jnp.maximum(s, 0))]))
    for active, source, target in copies:

        @pl.when(active)
        def _():
            pltpu.make_async_copy(source, target, sem).start()

    return copies


def wait_for(copies, sem):
    for active, source, target in copies:

        @pl.when(active)
        def _():
            pltpu.make_async_copy(source, target, sem).wait()


def gather_kernel(col_tiles, most, times, steps, table, *refs):
    outs, sems = refs[-3:-1], refs[-1]
    refs = refs[:-3]
    gathered = []
    for part in range(PARTS):
        masked, got = refs[2 * part : 2 * part + 2]
        count = len(times[part])
        direct, passed = refs[2 * PARTS : 2 * PARTS + count], refs[2 * PARTS + count : 2 * PARTS + 2 * count]
        refs = refs[: 2 * PARTS] + refs[2 * PARTS + 2 * count :]
        gathered.append(
            gather_panel(col_tiles, most, times[part], table, masked, got, direct, passed, outs[part], sems.at[part])
        )
    for part in range(PARTS):
        last = steps - PARTS + part
        for s, out in arrivals(table, most, [last], [outs[part]], [outs[part]]):

            @pl.when(s >= 0)
            def _():
                out[:, panel_columns(jnp.maximum(s, 0))] = jnp.zeros((out.shape[0], TILE), BF16)

    for part in range(PARTS):
        wait_for(gathered[part], sems.at[part])


def early_product_kernel(*refs):
    panels, right, outs = refs[:PARTS], refs[PARTS], refs[PARTS + 1 :]
    for left, out in zip(panels, outs):
        for i in range(right.shape[1] // TILE):
            columns = slice(i * TILE, (i + 1) * TILE)
            out[:, columns] = jnp.dot(left[...], right[:, columns], preferred_element_type=jnp.float32)


def add_last_kernel(most, t, table, early, right, direct, passed, *refs):
    out, result, sems = refs[-3:]
    part, height = t % PARTS, early.shape[0]
    (here, _), (there, _) = arrivals(table, most, [t], [direct], [passed])
    some, both = jnp.maximum(here, there) >= 0, jnp.minimum(here, there) >= 0

    def write(pieces):
        copies = []
        for i in range(result.shape[0]):
            columns = slice(i * TILE, (i + 1) * TILE)
            total = early[:, columns]
            for s, piece in pieces:
                total = total + jnp.dot(piece, right[panel_columns(s), columns], preferred_element_type=jnp.float32)
            result[i] = total.astype(BF16)
            target = out.at[part * height : (part + 1) * height, columns]
            copies.append(pltpu.make_async_copy(result.at[i], target, sems.at[i]))
            copies[i].start()
        for copy in copies:
            copy.wait()

    @pl.when(both)
    def _():
        write([(here, direct[...]), (there, passed[...])])

    @pl.when(some & jnp.logical_not(both))
    def _():
        write([(jnp.maximum(here, there), jnp.where(here >= 0, direct[...], passed[...]))])

    @pl.when(jnp.logical_not(some))
    def _():
        write([])


def mates(cols):
    return [(c, c ^ 1) for c in range(cols)]


def program(rows, cols, col_tiles, row_tiles, sizes, sections, table, *masked):
    steps, in_row, in_pair = sizes
    height, width = row_tiles * TILE, col_tiles * TILE
    chips = cols // CORES
    most = most_steps(chips)
    square = rows == 4
    tall = height // PARTS
    swap = mates(cols)
    ring = list(range(0, cols, CORES)) + list(range(cols - 1, 0, -CORES))
    around = [(ring[i], ring[(i + 1) % cols]) for i in range(cols)]
    rows_start = 3 * most + SECTIONS

    def stack(slots):
        return jax.ShapeDtypeStruct((slots, TILE, width), BF16)

    def turn(array, bits):
        pairs = [(r * cols + c, (r ^ bits[c % CORES]) * cols + c) for r in range(rows) for c in range(cols)]
        return lax.ppermute(array, ("row", "col"), pairs)

    got = [lax.ppermute(piece, "col", swap) for piece in masked]
    if square:
        own_rows = pl.pallas_call(
            functools.partial(own_rows_kernel, col_tiles, row_tiles, rows_start),
            out_shape=(stack(PAIR),) * (in_row // PAIR),
            in_specs=[VMEM] * (1 + PARTS),
            out_specs=(VMEM,) * (in_row // PAIR),
            compiler_params=PARAMS,
            name="own_rows",
        )(table, *masked)
        got_rows = [turn(own, (1, 2)) for own in own_rows]
    else:
        own_rows = pl.pallas_call(
            functools.partial(masked_rows_kernel, col_tiles, row_tiles),
            out_shape=stack(SECTIONS),
            in_specs=[SMEM] + [VMEM] * PARTS,
            out_specs=VMEM,
            compiler_params=PARAMS,
            name="masked_rows",
        )(sections, *masked)
        right = lax.psum(own_rows, "row")

    direct, passed = [], []
    for t in range(steps):
        operands = [table, masked[t % PARTS], got[t % PARTS]]
        specs = [VMEM] * len(operands)
        if t >= LAG:
            operands.append(direct[t - LAG])
            specs.append(VMEM)
        order = [sent] if t > 0 else []
        if t >= LAG + 2:
            order.append(passed[t - LAG - (2 if t < steps - 1 else 1)])
        if square and t == in_row + 1:
            order += got_rows
        operands += order
        specs += [ANY] * len(order)
        sent = pl.pallas_call(
            functools.partial(choose_kernel, col_tiles, t),
            out_shape=jax.ShapeDtypeStruct((tall, TILE), BF16),
            in_specs=specs,
            out_specs=VMEM,
            compiler_params=PARAMS,
            name="choose",
        )(*operands)
        if t >= LAG:
            sent, piece = lax.optimization_barrier((sent, direct[t - LAG]))
            passed.append(lax.ppermute(piece, "col", swap))
        direct.append(lax.ppermute(sent, "col", around))
    passed.append(lax.ppermute(direct[-2], "col", swap))

    if square:
        near = pl.pallas_call(
            functools.partial(near_rows_kernel, rows_start + SECTIONS),
            out_shape=stack(in_pair),
            in_specs=[VMEM] + [VMEM] * (2 * len(own_rows)) + [ANY],
            out_specs=VMEM,
            compiler_params=PARAMS,
            name="near_rows",
        )(table, *own_rows, *got_rows, direct[1 if in_row == PAIR else 2])
        right = pl.pallas_call(
            functools.partial(all_rows_kernel, rows_start + 2 * SECTIONS),
            out_shape=stack(SECTIONS),
            in_specs=[VMEM] * 3,
            out_specs=VMEM,
            compiler_params=PARAMS,
            name="all_rows",
        )(table, *lax.optimization_barrier((near, turn(near, (2, 1)), sent))[:2])
    right = right.reshape(SECTIONS * TILE, width)

    panel = jax.ShapeDtypeStruct((tall, SECTIONS * TILE), BF16)
    partial = jax.ShapeDtypeStruct((tall, width), jnp.float32)
    result = jax.ShapeDtypeStruct((height, width), BF16)
    buffers = [pltpu.VMEM((col_tiles, tall, TILE), BF16), pltpu.SemaphoreType.DMA((col_tiles,))]
    times = [list(range(part, steps - PARTS, PARTS)) for part in range(PARTS)]
    piece, right = lax.optimization_barrier((sent, right))
    operands = [array for part in range(PARTS) for array in (masked[part], got[part])]
    for part in range(PARTS):
        operands += [direct[t] for t in times[part]] + [passed[t] for t in times[part]]
    operands.append(piece)
    left = pl.pallas_call(
        functools.partial(gather_kernel, col_tiles, most, times, steps),
        out_shape=(panel,) * PARTS,
        in_specs=[VMEM] + [ANY] * len(operands),
        out_specs=(VMEM,) * PARTS,
        scratch_shapes=[pltpu.SemaphoreType.DMA((PARTS,))],
        compiler_params=PARAMS,
        name="gather",
    )(table, *operands)
    *left, right, direct[-2] = lax.optimization_barrier((*left, right, direct[-2]))
    early = pl.pallas_call(
        early_product_kernel,
        out_shape=(partial,) * PARTS,
        in_specs=[VMEM] * (PARTS + 1),
        out_specs=(VMEM,) * PARTS,
        compiler_params=PARAMS,
        name="early_product",
    )(*left, right)
    direct[-1], passed[-1], *early = lax.optimization_barrier((direct[-1], passed[-1], *early))
    passed.append(lax.ppermute(direct[-1], "col", swap))

    def add_last(t, before):
        return pl.pallas_call(
            functools.partial(add_last_kernel, most, t),
            out_shape=result,
            in_specs=[VMEM] * 5 + [HBM] * len(before),
            out_specs=HBM,
            input_output_aliases={5: 0} if before else {},
            scratch_shapes=buffers,
            compiler_params=PARAMS,
            name="add_last",
        )(table, early[t % PARTS], right, direct[t], passed[t], *before)

    return add_last(steps - 1, (add_last(steps - 2, ()),))


def shards(rows, cols, values, pattern, sections):
    row_tiles, col_tiles = pattern.shape
    height, width = values.shape
    chips = cols // CORES
    most = most_steps(chips)
    panel = jax.ShapeDtypeStruct((col_tiles, height // PARTS, TILE), BF16)
    *masked, table, which, chosen = pl.pallas_call(
        functools.partial(prepare_kernel, rows, col_tiles, row_tiles, chips),
        out_shape=(panel,) * PARTS
        + (
            jax.ShapeDtypeStruct((-(-(3 * most + 4 * SECTIONS) // 8) * 8, 128), jnp.int32),
            jax.ShapeDtypeStruct((1,), jnp.int32),
            jax.ShapeDtypeStruct(sections.shape, jnp.int32),
        ),
        in_specs=[HBM, HBM, HBM],
        out_specs=(VMEM,) * (PARTS + 1) + (SMEM, SMEM),
        scratch_shapes=[
            pltpu.SMEM(sections.shape, jnp.int32),
            pltpu.SMEM((col_tiles, row_tiles), jnp.int32),
            pltpu.SemaphoreType.DMA((col_tiles, row_tiles)),
            pltpu.SemaphoreType.DMA((2,)),
        ],
        compiler_params=pltpu.CompilerParams(vmem_limit_bytes=62 * 1024 * 1024),
        name="prepare",
    )(sections, pattern.T, values)
    branches = [
        functools.partial(program, rows, cols, col_tiles, row_tiles, sizes) for sizes in size_keys(rows, chips)
    ]
    return lax.switch(which[0], branches, chosen, table, *masked)


def solution(mesh):
    body = functools.partial(shards, mesh.shape["row"], mesh.shape["col"])
    in_specs = (P("row", "col"), P("row", "col"), P())
    return jax.shard_map(body, mesh=mesh, in_specs=in_specs, out_specs=P("row", "col"), check_vma=False)
```

```python
import functools

import jax
import jax.numpy as jnp
from jax import lax
from jax.experimental import pallas as pl
from jax.experimental.pallas import tpu as pltpu
from jax.sharding import PartitionSpec as P

TILE = 256
SECTIONS = 4
CORES = 2
PARTS = 2
LAG = 2
PAIR = 2
STRIP = 128
BLOCKS = 2
STEPS_A_WORD = 8
BF16 = jnp.bfloat16
ANY = pl.BlockSpec(memory_space=pl.ANY)
SMEM = pl.BlockSpec(memory_space=pltpu.SMEM)
VMEM = pl.BlockSpec(memory_space=pltpu.VMEM)
HBM = pl.BlockSpec(memory_space=pltpu.HBM)
PARAMS = pltpu.CompilerParams(vmem_limit_bytes=32 * 1024 * 1024)


def quotient(x, n):
    return lax.shift_right_logical(x, jnp.int32(n.bit_length() - 1)) if n & (n - 1) == 0 else lax.div(x, jnp.int32(n))


def remainder(x, n):
    return x & (n - 1) if n & (n - 1) == 0 else lax.rem(x, jnp.int32(n))


def slots(owners, chips):
    flows = [o < chips - 1 for o in owners]

    def ahead(i, s):
        return flows[i] & ((owners[i] >= owners[s]) if i < s else (owners[i] > owners[s]))

    ranks = [
        sum(ahead(i, s).astype(jnp.int32) for i in range(SECTIONS) if i != s) for s in range(SECTIONS)
    ]
    firsts = []
    steps = jnp.int32(0)
    for s in range(SECTIONS):
        first = -LAG * owners[s]
        for j in range(SECTIONS):
            if j != s:
                pushed = (ranks[s] - ranks[j]) * PARTS - LAG * owners[j]
                first = jnp.where(ahead(j, s), jnp.maximum(first, pushed), first)
        firsts.append(first)
        steps = jnp.where(flows[s], jnp.maximum(steps, first + PARTS + LAG * (chips - 2)), steps)
    return firsts, steps


def owners_of(sections, col_tiles):
    return [quotient(sections[s], col_tiles * CORES) for s in range(SECTIONS)]


def lines(sections, col_tiles, chips):
    owners = owners_of(sections, col_tiles)
    return owners, [chips - 1 - o for o in owners]


def most_steps(chips):
    return SECTIONS * PARTS + LAG * (chips - 2)


def size_keys(rows, chips):
    most = most_steps(chips)
    if rows != 4 or chips > 4:
        return [(most, SECTIONS, SECTIONS)]
    return [
        (most - (SECTIONS - count) * PARTS, PAIR if count <= PAIR else SECTIONS, min(count + 1, SECTIONS))
        for count in range(1, SECTIONS + 1)
    ]


def table_rows(chips):
    own = 3 * most_steps(chips)
    words = own + 4 * SECTIONS
    return own, words, words + 1 + 2 * -(-most_steps(chips) // STEPS_A_WORD)


def largest(values):
    return functools.reduce(jnp.maximum, values)


def prepare_kernel(rows, col_tiles, row_tiles, chips, sections_in, pattern_in, values, *refs):
    masked = refs[:PARTS]
    table, which, sections, pattern, sems, small = refs[PARTS:]
    height = row_tiles * TILE // PARTS
    col = lax.axis_index("col")
    chip, core = quotient(col, CORES), remainder(col, CORES)
    most = most_steps(chips)

    def fetch(r):
        part, start = r * TILE // height, r * TILE % height
        block = values.at[r * TILE : (r + 1) * TILE, :]
        return pltpu.make_async_copy(block, masked[part].at[start : start + TILE, :], sems.at[r])

    lists = [
        pltpu.make_async_copy(sections_in, sections, small.at[0]),
        pltpu.make_async_copy(pattern_in, pattern, small.at[1]),
    ]
    for copy in lists:
        copy.start()
    for r in range(row_tiles):
        fetch(r).start()
    table[...] = jnp.full(table.shape, -1, jnp.int32)

    def note(row, item):
        table[pl.ds(row, 1), :] = jnp.full((1, table.shape[1]), item, jnp.int32)

    for copy in lists:
        copy.wait()
    up, down = lines(sections, col_tiles, chips)
    needed = jnp.int32(0)
    in_flow = [[jnp.int32(0)] * -(-most // STEPS_A_WORD) for _ in range(2)]
    for flow, line in enumerate((up, down)):
        place = chip if flow == 0 else chips - 1 - chip
        firsts, steps = slots(line, chips)
        needed = jnp.maximum(needed, steps)
        mine = core == flow
        for s in range(SECTIONS):

            @pl.when(mine & (line[s] == place) & (line[s] < chips - 1))
            def _():
                local = sections[s] - up[s] * (col_tiles * CORES)
                for part in range(PARTS):
                    note(firsts[s] + LAG * place + part, local)

            begin = firsts[s] + LAG * (place - 1)
            pair = (s + 1) * 17 << 4 * remainder(begin, STEPS_A_WORD)
            for word in range(len(in_flow[flow])):
                inside = (line[s] < place) & (quotient(begin, STEPS_A_WORD) == word)
                in_flow[flow][word] = in_flow[flow][word] + jnp.where(inside, pair, 0)

            @pl.when(line[s] < place)
            def _():
                for part in range(PARTS):
                    note(jnp.where(mine, most, 2 * most) + firsts[s] + LAG * (place - 1) + part, s)

    for s in range(SECTIONS):

        @pl.when(up[s] == chip)
        def _():
            note(3 * most + s, sections[s] - up[s] * (col_tiles * CORES))

    _, words, _ = table_rows(chips)
    tiles = jnp.int32(0)
    for s in range(SECTIONS):
        tiles = tiles + jnp.where(up[s] == chip, sections[s] - up[s] * (col_tiles * CORES) + 1 << 4 * s, 0)
    note(words, tiles)
    for word, (first, second) in enumerate(zip(*in_flow)):
        note(words + 1 + 2 * word, jnp.where(core == 0, first, second))
        note(words + 2 + 2 * word, jnp.where(core == 0, second, first))
    if rows == 4:
        note_rows(note, 3 * most + SECTIONS, sections, row_tiles, core)
    keys = size_keys(rows, chips)
    number = jnp.int32(0)
    if len(keys) > 1:
        owners = [quotient(sections[s], row_tiles) for s in range(SECTIONS)]
        counts = [sum((o == r).astype(jnp.int32) for o in owners) for r in range(4)]
        in_row = largest(counts)
        in_pair = largest([counts[i] + counts[j] for i, j in ((0, 1), (2, 3), (0, 2), (1, 3))])
        for key in keys[:-1]:
            fits = (needed <= key[0]) & (in_row <= key[1]) & (in_pair <= key[2])
            number = number + jnp.where(fits, 0, 1)
    which[0] = number

    for r in range(row_tiles):
        fetch(r).wait()
        part, start = r * TILE // height, r * TILE % height
        for c in range(col_tiles):

            @pl.when(pattern[c, r] == 0)
            def _():
                masked[part][start : start + TILE, c * TILE : (c + 1) * TILE] = jnp.zeros((TILE, TILE), BF16)


def rank_among(owners, s):
    return sum((owners[i] == owners[s]).astype(jnp.int32) for i in range(s)) + jnp.int32(0)


def bits(owner, first):
    x, y = remainder(owner, 2), quotient(owner, 2)
    return jnp.where(first, x, y), jnp.where(first, y, x)


def note_rows(note, start, sections, row_tiles, core):
    row = lax.axis_index("row")
    first = core == 0
    here = bits(row, first)
    owners = [quotient(sections[s], row_tiles) for s in range(SECTIONS)]
    pairs = [bits(o, first)[1] for o in owners]
    for s in range(SECTIONS):
        rank, slot = rank_among(owners, s), rank_among(pairs, s)

        @pl.when(owners[s] == row)
        def _():
            note(start + rank, sections[s] - owners[s] * row_tiles)

        @pl.when(pairs[s] == here[1])
        def _():
            note(start + SECTIONS + slot, rank + jnp.where(bits(owners[s], first)[0] == here[0], 0, SECTIONS))

        note(start + 2 * SECTIONS + s, slot + jnp.where(pairs[s] == here[1], 0, SECTIONS))


def own_rows_kernel(col_tiles, row_tiles, start, table, *refs):
    masked, outs = refs[:PARTS], refs[PARTS:]
    in_part = row_tiles // PARTS
    places = [(out, place) for out in outs for place in range(PAIR)]
    tiles = [jnp.max(table[start + i : start + i + 1, :]) for i in range(len(places))]
    for (out, place), tile in zip(places, tiles):
        local = jnp.maximum(tile, 0)
        for part in range(PARTS):
            first = pl.multiple_of((local - part * in_part) * TILE, TILE)

            @pl.when((tile >= 0) & (quotient(local, in_part) == part))
            def _():
                out[place] = masked[part][pl.ds(first, TILE), :]


def masked_rows_kernel(col_tiles, row_tiles, sections, *refs):
    masked, out = refs[:PARTS], refs[-1]
    row = lax.axis_index("row")
    in_part = row_tiles // PARTS
    for s in range(SECTIONS):
        owner = quotient(sections[s], row_tiles)
        local = sections[s] - owner * row_tiles
        out[s] = jnp.zeros(out.shape[1:], BF16)
        for part in range(PARTS):
            first = pl.multiple_of((local - part * in_part) * TILE, TILE)

            @pl.when((owner == row) & (quotient(local, in_part) == part))
            def _():
                out[s] = masked[part][pl.ds(first, TILE), :]


def near_rows_kernel(start, table, *refs):
    out = refs[-1]
    arrays = len(refs) // 2 - 1
    own, got = refs[:arrays], refs[arrays : 2 * arrays]
    sources = [jnp.max(table[start + i : start + i + 1, :]) for i in range(out.shape[0])]
    for i, source in enumerate(sources):
        rank = remainder(jnp.maximum(source, 0), SECTIONS)
        place = remainder(rank, PAIR)
        for number in range(arrays):
            wanted = (source >= 0) & (quotient(rank, PAIR) == number)

            @pl.when(wanted & (source < SECTIONS))
            def _():
                out[i] = own[number][place]

            @pl.when(wanted & (source >= SECTIONS))
            def _():
                out[i] = got[number][place]


def all_rows_kernel(start, table, near, far, out):
    sources = [jnp.max(table[start + s : start + s + 1, :]) for s in range(SECTIONS)]
    for s, source in enumerate(sources):
        slot = remainder(source, SECTIONS)

        @pl.when(source < SECTIONS)
        def _():
            out[s] = near[slot]

        @pl.when(source >= SECTIONS)
        def _():
            out[s] = far[slot]


def choose_kernel(col_tiles, t, table, masked, got, *refs):
    out = refs[-1]
    core = remainder(lax.axis_index("col"), CORES)
    tile = jnp.max(table[t : t + 1, :])
    local, owner = remainder(jnp.maximum(tile, 0), col_tiles), quotient(jnp.maximum(tile, 0), col_tiles)

    everything = slice(0, TILE)

    @pl.when((tile >= 0) & (owner == core))
    def _():
        copy_strips(masked, panel_columns(local), out, everything)

    @pl.when((tile >= 0) & (owner != core))
    def _():
        copy_strips(got, panel_columns(local), out, everything)

    if t >= LAG:

        @pl.when(tile < 0)
        def _():
            copy_strips(refs[0], everything, out, everything)


def panel_columns(s):
    return pl.ds(pl.multiple_of(s * TILE, TILE), TILE)


def arrivals(table, most, times, direct, passed):
    rows = [(entry * most + t, source) for t, d, p in zip(times, direct, passed) for entry, source in ((1, d), (2, p))]
    return [(jnp.max(table[row : row + 1, :]), source) for row, source in rows]


def copy_strips(source, taken, target, columns):
    @pl.loop(0, source.shape[0] // STRIP)
    def _(i):
        strip = pl.ds(pl.multiple_of(i * STRIP, STRIP), STRIP)
        target[strip, columns] = source[strip, taken]


def gather_kernel(col_tiles, chips, times, steps, table, *refs):
    refs, outs = refs[:-PARTS], refs[-PARTS:]
    core = remainder(lax.axis_index("col"), CORES)
    _, words, _ = table_rows(chips)
    tiles = jnp.max(table[words : words + 1, :])
    packed = [jnp.max(table[row : row + 1, :]) for row in range(words + 1, words + 1 + 2 * -(-steps // STEPS_A_WORD))]

    def entry(way, t):
        shift = jnp.int32(4 * (t % STEPS_A_WORD))
        return (lax.shift_right_logical(packed[2 * (t // STEPS_A_WORD) + way], shift) & 15) - 1

    for part in range(PARTS):
        masked, got = refs[2 * part : 2 * part + 2]
        count = len(times[part])
        ways = refs[2 * PARTS : 2 * PARTS + count], refs[2 * PARTS + count : 2 * PARTS + 2 * count]
        refs = refs[: 2 * PARTS] + refs[2 * PARTS + 2 * count :]
        left = outs[part]
        for s in range(SECTIONS):
            tile = (lax.shift_right_logical(tiles, jnp.int32(4 * s)) & 15) - 1
            local, owner = remainder(jnp.maximum(tile, 0), col_tiles), quotient(jnp.maximum(tile, 0), col_tiles)
            columns = slice(s * TILE, (s + 1) * TILE)

            @pl.when((tile >= 0) & (owner == core))
            def _():
                copy_strips(masked, panel_columns(local), left, columns)

            @pl.when((tile >= 0) & (owner != core))
            def _():
                copy_strips(got, panel_columns(local), left, columns)

        for way in range(2):
            for t, source in zip(times[part], ways[way]):
                s = entry(way, t)

                @pl.when(s >= 0)
                def _():
                    copy_strips(source, slice(0, TILE), left, panel_columns(jnp.maximum(s, 0)))

            s = entry(way, steps - PARTS + part)

            @pl.when(s >= 0)
            def _():
                left[:, panel_columns(jnp.maximum(s, 0))] = jnp.zeros((left.shape[0], TILE), BF16)


def early_product_kernel(*refs):
    panels, right, outs = refs[:PARTS], refs[PARTS], refs[PARTS + 1 :]
    for left, out in zip(panels, outs):
        for i in range(right.shape[1] // TILE):
            columns = slice(i * TILE, (i + 1) * TILE)
            out[:, columns] = jnp.dot(left[...], right[:, columns], preferred_element_type=jnp.float32)


def add_last_kernel(most, t, table, early, right, direct, passed, *refs):
    out, result, sems = refs[-3:]
    part, height = t % PARTS, early.shape[0]
    (here, _), (there, _) = arrivals(table, most, [t], [direct], [passed])
    some, both = jnp.maximum(here, there) >= 0, jnp.minimum(here, there) >= 0

    def write(pieces):
        copies = []
        for i in range(result.shape[0]):
            columns = slice(i * TILE, (i + 1) * TILE)
            for k in range(BLOCKS):
                rows = slice(k * (height // BLOCKS), (k + 1) * (height // BLOCKS))
                total = early[rows, columns]
                for s, piece in pieces:
                    total = total + jnp.dot(
                        piece[rows, :], right[panel_columns(s), columns], preferred_element_type=jnp.float32
                    )
                result[i, rows, :] = total.astype(BF16)
                target = out.at[part * height + rows.start : part * height + rows.stop, columns]
                copies.append(pltpu.make_async_copy(result.at[i, rows, :], target, sems.at[i, k]))
                copies[-1].start()
        for copy in copies:
            copy.wait()

    @pl.when(both)
    def _():
        write([(here, direct[...]), (there, passed[...])])

    @pl.when(some & jnp.logical_not(both))
    def _():
        write([(jnp.maximum(here, there), jnp.where(here >= 0, direct[...], passed[...]))])

    @pl.when(jnp.logical_not(some))
    def _():
        write([])


def mates(cols):
    return [(c, c ^ 1) for c in range(cols)]


def program(rows, cols, col_tiles, row_tiles, sizes, sections, table, *masked):
    steps, in_row, in_pair = sizes
    height, width = row_tiles * TILE, col_tiles * TILE
    chips = cols // CORES
    most = most_steps(chips)
    square = rows == 4
    tall = height // PARTS
    swap = mates(cols)
    ring = list(range(0, cols, CORES)) + list(range(cols - 1, 0, -CORES))
    around = [(ring[i], ring[(i + 1) % cols]) for i in range(cols)]
    rows_start = 3 * most + SECTIONS

    def stack(slots):
        return jax.ShapeDtypeStruct((slots, TILE, width), BF16)

    def turn(array, bits):
        pairs = [(r * cols + c, (r ^ bits[c % CORES]) * cols + c) for r in range(rows) for c in range(cols)]
        return lax.ppermute(array, ("row", "col"), pairs)

    got = [lax.ppermute(piece, "col", swap) for piece in masked]
    if square:
        own_rows = pl.pallas_call(
            functools.partial(own_rows_kernel, col_tiles, row_tiles, rows_start),
            out_shape=(stack(PAIR),) * (in_row // PAIR),
            in_specs=[VMEM] * (1 + PARTS),
            out_specs=(VMEM,) * (in_row // PAIR),
            compiler_params=PARAMS,
            name="own_rows",
        )(table, *masked)
        got_rows = [turn(own, (1, 2)) for own in own_rows]
    else:
        own_rows = pl.pallas_call(
            functools.partial(masked_rows_kernel, col_tiles, row_tiles),
            out_shape=stack(SECTIONS),
            in_specs=[SMEM] + [VMEM] * PARTS,
            out_specs=VMEM,
            compiler_params=PARAMS,
            name="masked_rows",
        )(sections, *masked)
        right = lax.psum(own_rows, "row")

    direct, passed = [], []
    for t in range(steps):
        operands = [table, masked[t % PARTS], got[t % PARTS]]
        specs = [VMEM] * len(operands)
        if t >= LAG:
            operands.append(direct[t - LAG])
            specs.append(VMEM)
        order = [sent] if t > 0 else []
        if t >= LAG + 2:
            order.append(passed[t - LAG - (1 if t == steps - 1 and in_row == PAIR else 2)])
        if square and t == in_row + 1:
            order += got_rows
        operands += order
        specs += [ANY] * len(order)
        sent = pl.pallas_call(
            functools.partial(choose_kernel, col_tiles, t),
            out_shape=jax.ShapeDtypeStruct((tall, TILE), BF16),
            in_specs=specs,
            out_specs=VMEM,
            compiler_params=PARAMS,
            name="choose",
        )(*operands)
        if t >= LAG:
            sent, piece = lax.optimization_barrier((sent, direct[t - LAG]))
            passed.append(lax.ppermute(piece, "col", swap))
        direct.append(lax.ppermute(sent, "col", around))
    passed.append(lax.ppermute(direct[-2], "col", swap))

    if square:
        near = pl.pallas_call(
            functools.partial(near_rows_kernel, rows_start + SECTIONS),
            out_shape=stack(in_pair),
            in_specs=[VMEM] + [VMEM] * (2 * len(own_rows)) + [ANY],
            out_specs=VMEM,
            compiler_params=PARAMS,
            name="near_rows",
        )(table, *own_rows, *got_rows, direct[1 if in_row == PAIR else 2])
        right = pl.pallas_call(
            functools.partial(all_rows_kernel, rows_start + 2 * SECTIONS),
            out_shape=stack(SECTIONS),
            in_specs=[VMEM] * 3,
            out_specs=VMEM,
            compiler_params=PARAMS,
            name="all_rows",
        )(table, *lax.optimization_barrier((near, turn(near, (2, 1)), sent))[:2])
    right = right.reshape(SECTIONS * TILE, width)

    panel = jax.ShapeDtypeStruct((tall, SECTIONS * TILE), BF16)
    partial = jax.ShapeDtypeStruct((tall, width), jnp.float32)
    result = jax.ShapeDtypeStruct((height, width), BF16)
    buffers = [pltpu.VMEM((col_tiles, tall, TILE), BF16), pltpu.SemaphoreType.DMA((col_tiles, BLOCKS))]
    times = [list(range(part, steps - PARTS, PARTS)) for part in range(PARTS)]
    piece, right = lax.optimization_barrier((sent, right))
    operands = [array for part in range(PARTS) for array in (masked[part], got[part])]
    for part in range(PARTS):
        operands += [direct[t] for t in times[part]] + [passed[t] for t in times[part]]
    operands.append(piece)
    left = pl.pallas_call(
        functools.partial(gather_kernel, col_tiles, chips, times, steps),
        out_shape=(panel,) * PARTS,
        in_specs=[VMEM] * len(operands) + [ANY],
        out_specs=(VMEM,) * PARTS,
        compiler_params=PARAMS,
        name="gather",
    )(table, *operands)
    *left, right, direct[-2] = lax.optimization_barrier((*left, right, direct[-2]))
    early = pl.pallas_call(
        early_product_kernel,
        out_shape=(partial,) * PARTS,
        in_specs=[VMEM] * (PARTS + 1),
        out_specs=(VMEM,) * PARTS,
        compiler_params=PARAMS,
        name="early_product",
    )(*left, right)
    direct[-1], passed[-1], *early = lax.optimization_barrier((direct[-1], passed[-1], *early))
    passed.append(lax.ppermute(direct[-1], "col", swap))

    def add_last(t, before):
        return pl.pallas_call(
            functools.partial(add_last_kernel, most, t),
            out_shape=result,
            in_specs=[VMEM] * 5 + [HBM] * len(before),
            out_specs=HBM,
            input_output_aliases={5: 0} if before else {},
            scratch_shapes=buffers,
            compiler_params=PARAMS,
            name="add_last",
        )(table, early[t % PARTS], right, direct[t], passed[t], *before)

    return add_last(steps - 1, (add_last(steps - 2, ()),))


def shards(rows, cols, values, pattern, sections):
    row_tiles, col_tiles = pattern.shape
    height, width = values.shape
    chips = cols // CORES
    most = most_steps(chips)
    panel = jax.ShapeDtypeStruct((height // PARTS, width), BF16)
    *masked, table, which = pl.pallas_call(
        functools.partial(prepare_kernel, rows, col_tiles, row_tiles, chips),
        out_shape=(panel,) * PARTS
        + (
            jax.ShapeDtypeStruct((-(-table_rows(chips)[2] // 8) * 8, 128), jnp.int32),
            jax.ShapeDtypeStruct((1,), jnp.int32),
        ),
        in_specs=[HBM, HBM, HBM],
        out_specs=(VMEM,) * (PARTS + 1) + (SMEM,),
        scratch_shapes=[
            pltpu.SMEM(sections.shape, jnp.int32),
            pltpu.SMEM((col_tiles, row_tiles), jnp.int32),
            pltpu.SemaphoreType.DMA((row_tiles,)),
            pltpu.SemaphoreType.DMA((2,)),
        ],
        compiler_params=pltpu.CompilerParams(vmem_limit_bytes=62 * 1024 * 1024),
        name="prepare",
    )(sections, pattern.T, values)
    branches = [
        functools.partial(program, rows, cols, col_tiles, row_tiles, sizes) for sizes in size_keys(rows, chips)
    ]
    return lax.switch(which[0], branches, sections, table, *masked)


def solution(mesh):
    body = functools.partial(shards, mesh.shape["row"], mesh.shape["col"])
    in_specs = (P("row", "col"), P("row", "col"), P())
    return jax.shard_map(body, mesh=mesh, in_specs=in_specs, out_specs=P("row", "col"), check_vma=False)
```

```python
import functools

import jax
import jax.numpy as jnp
from jax import lax
from jax.experimental import pallas as pl
from jax.experimental.pallas import tpu as pltpu
from jax.sharding import PartitionSpec as P

TILE = 256
SECTIONS = 4
CORES = 2
PARTS = 2
LAG = 2
PAIR = 2
STRIP = 128
BLOCKS = 2
STEPS_A_WORD = 8
BF16 = jnp.bfloat16
ANY = pl.BlockSpec(memory_space=pl.ANY)
SMEM = pl.BlockSpec(memory_space=pltpu.SMEM)
VMEM = pl.BlockSpec(memory_space=pltpu.VMEM)
HBM = pl.BlockSpec(memory_space=pltpu.HBM)
PARAMS = pltpu.CompilerParams(vmem_limit_bytes=32 * 1024 * 1024)


def quotient(x, n):
    return lax.shift_right_logical(x, jnp.int32(n.bit_length() - 1)) if n & (n - 1) == 0 else lax.div(x, jnp.int32(n))


def remainder(x, n):
    return x & (n - 1) if n & (n - 1) == 0 else lax.rem(x, jnp.int32(n))


def slots(owners, chips):
    flows = [o < chips - 1 for o in owners]

    def ahead(i, s):
        return flows[i] & ((owners[i] >= owners[s]) if i < s else (owners[i] > owners[s]))

    ranks = [
        sum(ahead(i, s).astype(jnp.int32) for i in range(SECTIONS) if i != s) for s in range(SECTIONS)
    ]
    firsts = []
    steps = jnp.int32(0)
    for s in range(SECTIONS):
        first = -LAG * owners[s]
        for j in range(SECTIONS):
            if j != s:
                pushed = (ranks[s] - ranks[j]) * PARTS - LAG * owners[j]
                first = jnp.where(ahead(j, s), jnp.maximum(first, pushed), first)
        firsts.append(first)
        steps = jnp.where(flows[s], jnp.maximum(steps, first + PARTS + LAG * (chips - 2)), steps)
    return firsts, steps


def owners_of(sections, col_tiles):
    return [quotient(sections[s], col_tiles * CORES) for s in range(SECTIONS)]


def lines(sections, col_tiles, chips):
    owners = owners_of(sections, col_tiles)
    return owners, [chips - 1 - o for o in owners]


def most_steps(chips):
    return SECTIONS * PARTS + LAG * (chips - 2)


def size_keys(rows, chips):
    most = most_steps(chips)
    if rows != 4 or chips > 4:
        return [(most, SECTIONS, SECTIONS)]
    return [
        (most - (SECTIONS - count) * PARTS, PAIR if count <= PAIR else SECTIONS, min(count + 1, SECTIONS))
        for count in range(1, SECTIONS + 1)
    ]


def table_rows(chips):
    own = 3 * most_steps(chips)
    words = own + 4 * SECTIONS
    return own, words, words + 1 + 2 * -(-most_steps(chips) // STEPS_A_WORD)


def largest(values):
    return functools.reduce(jnp.maximum, values)


def prepare_kernel(rows, col_tiles, row_tiles, chips, sections_in, pattern_in, values, *refs):
    masked = refs[:PARTS]
    table, which, sections, pattern, sems, small = refs[PARTS:]
    height = row_tiles * TILE // PARTS
    col = lax.axis_index("col")
    chip, core = quotient(col, CORES), remainder(col, CORES)
    most = most_steps(chips)

    def fetch(r):
        part, start = r * TILE // height, r * TILE % height
        block = values.at[r * TILE : (r + 1) * TILE, :]
        return pltpu.make_async_copy(block, masked[part].at[start : start + TILE, :], sems.at[r])

    lists = [
        pltpu.make_async_copy(sections_in, sections, small.at[0]),
        pltpu.make_async_copy(pattern_in, pattern, small.at[1]),
    ]
    for copy in lists:
        copy.start()
    for r in range(row_tiles):
        fetch(r).start()
    table[...] = jnp.full(table.shape, -1, jnp.int32)

    def note(row, item):
        table[pl.ds(row, 1), :] = jnp.full((1, table.shape[1]), item, jnp.int32)

    for copy in lists:
        copy.wait()
    up, down = lines(sections, col_tiles, chips)
    needed = jnp.int32(0)
    in_flow = [[jnp.int32(0)] * -(-most // STEPS_A_WORD) for _ in range(2)]
    for flow, line in enumerate((up, down)):
        place = chip if flow == 0 else chips - 1 - chip
        firsts, steps = slots(line, chips)
        needed = jnp.maximum(needed, steps)
        mine = core == flow
        for s in range(SECTIONS):

            @pl.when(mine & (line[s] == place) & (line[s] < chips - 1))
            def _():
                local = sections[s] - up[s] * (col_tiles * CORES)
                for part in range(PARTS):
                    note(firsts[s] + LAG * place + part, local)

            begin = firsts[s] + LAG * (place - 1)
            pair = (s + 1) * 17 << 4 * remainder(begin, STEPS_A_WORD)
            for word in range(len(in_flow[flow])):
                inside = (line[s] < place) & (quotient(begin, STEPS_A_WORD) == word)
                in_flow[flow][word] = in_flow[flow][word] + jnp.where(inside, pair, 0)

            @pl.when(line[s] < place)
            def _():
                for part in range(PARTS):
                    note(jnp.where(mine, most, 2 * most) + firsts[s] + LAG * (place - 1) + part, s)

    for s in range(SECTIONS):

        @pl.when(up[s] == chip)
        def _():
            note(3 * most + s, sections[s] - up[s] * (col_tiles * CORES))

    _, words, _ = table_rows(chips)
    tiles = jnp.int32(0)
    for s in range(SECTIONS):
        tiles = tiles + jnp.where(up[s] == chip, sections[s] - up[s] * (col_tiles * CORES) + 1 << 4 * s, 0)
    note(words, tiles)
    for word, (first, second) in enumerate(zip(*in_flow)):
        note(words + 1 + 2 * word, jnp.where(core == 0, first, second))
        note(words + 2 + 2 * word, jnp.where(core == 0, second, first))
    if rows == 4:
        note_rows(note, 3 * most + SECTIONS, sections, row_tiles, core)
    keys = size_keys(rows, chips)
    number = jnp.int32(0)
    if len(keys) > 1:
        owners = [quotient(sections[s], row_tiles) for s in range(SECTIONS)]
        counts = [sum((o == r).astype(jnp.int32) for o in owners) for r in range(4)]
        in_row = largest(counts)
        in_pair = largest([counts[i] + counts[j] for i, j in ((0, 1), (2, 3), (0, 2), (1, 3))])
        for key in keys[:-1]:
            fits = (needed <= key[0]) & (in_row <= key[1]) & (in_pair <= key[2])
            number = number + jnp.where(fits, 0, 1)
    which[0] = number

    for r in range(row_tiles):
        fetch(r).wait()
        part, start = r * TILE // height, r * TILE % height
        for c in range(col_tiles):

            @pl.when(pattern[c, r] == 0)
            def _():
                masked[part][start : start + TILE, c * TILE : (c + 1) * TILE] = jnp.zeros((TILE, TILE), BF16)


def rank_among(owners, s):
    return sum((owners[i] == owners[s]).astype(jnp.int32) for i in range(s)) + jnp.int32(0)


def bits(owner, first):
    x, y = remainder(owner, 2), quotient(owner, 2)
    return jnp.where(first, x, y), jnp.where(first, y, x)


def note_rows(note, start, sections, row_tiles, core):
    row = lax.axis_index("row")
    first = core == 0
    here = bits(row, first)
    owners = [quotient(sections[s], row_tiles) for s in range(SECTIONS)]
    pairs = [bits(o, first)[1] for o in owners]
    for s in range(SECTIONS):
        rank, slot = rank_among(owners, s), rank_among(pairs, s)

        @pl.when(owners[s] == row)
        def _():
            note(start + rank, sections[s] - owners[s] * row_tiles)

        @pl.when(pairs[s] == here[1])
        def _():
            note(start + SECTIONS + slot, rank + jnp.where(bits(owners[s], first)[0] == here[0], 0, SECTIONS))

        note(start + 2 * SECTIONS + s, slot + jnp.where(pairs[s] == here[1], 0, SECTIONS))


def own_rows_kernel(col_tiles, row_tiles, start, table, *refs):
    masked, outs = refs[:PARTS], refs[PARTS:]
    in_part = row_tiles // PARTS
    places = [(out, place) for out in outs for place in range(PAIR)]
    tiles = [jnp.max(table[start + i : start + i + 1, :1]) for i in range(len(places))]
    for (out, place), tile in zip(places, tiles):
        local = jnp.maximum(tile, 0)
        for part in range(PARTS):
            first = pl.multiple_of((local - part * in_part) * TILE, TILE)

            @pl.when((tile >= 0) & (quotient(local, in_part) == part))
            def _():
                out[place] = masked[part][pl.ds(first, TILE), :]


def masked_rows_kernel(col_tiles, row_tiles, sections, *refs):
    masked, out = refs[:PARTS], refs[-1]
    row = lax.axis_index("row")
    in_part = row_tiles // PARTS
    for s in range(SECTIONS):
        owner = quotient(sections[s], row_tiles)
        local = sections[s] - owner * row_tiles
        out[s] = jnp.zeros(out.shape[1:], BF16)
        for part in range(PARTS):
            first = pl.multiple_of((local - part * in_part) * TILE, TILE)

            @pl.when((owner == row) & (quotient(local, in_part) == part))
            def _():
                out[s] = masked[part][pl.ds(first, TILE), :]


def near_rows_kernel(start, table, *refs):
    out = refs[-1]
    arrays = len(refs) // 2 - 1
    own, got = refs[:arrays], refs[arrays : 2 * arrays]
    sources = [jnp.max(table[start + i : start + i + 1, :1]) for i in range(out.shape[0])]
    for i, source in enumerate(sources):
        rank = remainder(jnp.maximum(source, 0), SECTIONS)
        place = remainder(rank, PAIR)
        for number in range(arrays):
            wanted = (source >= 0) & (quotient(rank, PAIR) == number)

            @pl.when(wanted & (source < SECTIONS))
            def _():
                out[i] = own[number][place]

            @pl.when(wanted & (source >= SECTIONS))
            def _():
                out[i] = got[number][place]


def all_rows_kernel(start, table, near, far, out):
    sources = [jnp.max(table[start + s : start + s + 1, :1]) for s in range(SECTIONS)]
    for s, source in enumerate(sources):
        slot = remainder(source, SECTIONS)

        @pl.when(source < SECTIONS)
        def _():
            out[s] = near[slot]

        @pl.when(source >= SECTIONS)
        def _():
            out[s] = far[slot]


def choose_kernel(col_tiles, t, table, masked, got, *refs):
    out = refs[-1]
    core = remainder(lax.axis_index("col"), CORES)
    tile = jnp.max(table[t : t + 1, :1])
    local, owner = remainder(jnp.maximum(tile, 0), col_tiles), quotient(jnp.maximum(tile, 0), col_tiles)

    everything = slice(0, TILE)

    @pl.when((tile >= 0) & (owner == core))
    def _():
        copy_strips(masked, panel_columns(local), out, everything)

    @pl.when((tile >= 0) & (owner != core))
    def _():
        copy_strips(got, panel_columns(local), out, everything)

    if t >= LAG:

        @pl.when(tile < 0)
        def _():
            copy_strips(refs[0], everything, out, everything)


def panel_columns(s):
    return pl.ds(pl.multiple_of(s * TILE, TILE), TILE)


def arrivals(table, most, times, direct, passed):
    rows = [(entry * most + t, source) for t, d, p in zip(times, direct, passed) for entry, source in ((1, d), (2, p))]
    return [(jnp.max(table[row : row + 1, :1]), source) for row, source in rows]


def copy_strips(source, taken, target, columns):
    @pl.loop(0, source.shape[0] // STRIP)
    def _(i):
        strip = pl.ds(pl.multiple_of(i * STRIP, STRIP), STRIP)
        target[strip, columns] = source[strip, taken]


def gather_kernel(col_tiles, chips, times, steps, table, *refs):
    refs, outs = refs[:-PARTS], refs[-PARTS:]
    core = remainder(lax.axis_index("col"), CORES)
    _, words, _ = table_rows(chips)
    tiles = jnp.max(table[words : words + 1, :1])
    packed = [jnp.max(table[row : row + 1, :1]) for row in range(words + 1, words + 1 + 2 * -(-steps // STEPS_A_WORD))]

    def entry(way, t):
        shift = jnp.int32(4 * (t % STEPS_A_WORD))
        return (lax.shift_right_logical(packed[2 * (t // STEPS_A_WORD) + way], shift) & 15) - 1

    for part in range(PARTS):
        masked, got = refs[2 * part : 2 * part + 2]
        count = len(times[part])
        ways = refs[2 * PARTS : 2 * PARTS + count], refs[2 * PARTS + count : 2 * PARTS + 2 * count]
        refs = refs[: 2 * PARTS] + refs[2 * PARTS + 2 * count :]
        left = outs[part]
        for s in range(SECTIONS):
            tile = (lax.shift_right_logical(tiles, jnp.int32(4 * s)) & 15) - 1
            local, owner = remainder(jnp.maximum(tile, 0), col_tiles), quotient(jnp.maximum(tile, 0), col_tiles)
            columns = slice(s * TILE, (s + 1) * TILE)

            @pl.when((tile >= 0) & (owner == core))
            def _():
                copy_strips(masked, panel_columns(local), left, columns)

            @pl.when((tile >= 0) & (owner != core))
            def _():
                copy_strips(got, panel_columns(local), left, columns)

        for way in range(2):
            for t, source in zip(times[part], ways[way]):
                s = entry(way, t)

                @pl.when(s >= 0)
                def _():
                    copy_strips(source, slice(0, TILE), left, panel_columns(jnp.maximum(s, 0)))

            s = entry(way, steps - PARTS + part)

            @pl.when(s >= 0)
            def _():
                left[:, panel_columns(jnp.maximum(s, 0))] = jnp.zeros((left.shape[0], TILE), BF16)


def early_product_kernel(*refs):
    panels, right, outs = refs[:PARTS], refs[PARTS], refs[PARTS + 1 :]
    for left, out in zip(panels, outs):
        for i in range(right.shape[1] // TILE):
            columns = slice(i * TILE, (i + 1) * TILE)
            out[:, columns] = jnp.dot(left[...], right[:, columns], preferred_element_type=jnp.float32)


def add_last_kernel(most, t, table, early, right, direct, passed, *refs):
    out, result, sems = refs[-3:]
    part, height = t % PARTS, early.shape[0]
    (here, _), (there, _) = arrivals(table, most, [t], [direct], [passed])
    some, both = jnp.maximum(here, there) >= 0, jnp.minimum(here, there) >= 0

    def write(pieces):
        copies = []
        for i in range(result.shape[0]):
            columns = slice(i * TILE, (i + 1) * TILE)
            for k in range(BLOCKS):
                rows = slice(k * (height // BLOCKS), (k + 1) * (height // BLOCKS))
                total = early[rows, columns]
                for s, piece in pieces:
                    total = total + jnp.dot(
                        piece[rows, :], right[panel_columns(s), columns], preferred_element_type=jnp.float32
                    )
                result[i, rows, :] = total.astype(BF16)
                target = out.at[part * height + rows.start : part * height + rows.stop, columns]
                copies.append(pltpu.make_async_copy(result.at[i, rows, :], target, sems.at[i, k]))
                copies[-1].start()
        for copy in copies:
            copy.wait()

    @pl.when(both)
    def _():
        write([(here, direct[...]), (there, passed[...])])

    @pl.when(some & jnp.logical_not(both))
    def _():
        write([(jnp.maximum(here, there), jnp.where(here >= 0, direct[...], passed[...]))])

    @pl.when(jnp.logical_not(some))
    def _():
        write([])


def mates(cols):
    return [(c, c ^ 1) for c in range(cols)]


def program(rows, cols, col_tiles, row_tiles, sizes, sections, table, *masked):
    steps, in_row, in_pair = sizes
    height, width = row_tiles * TILE, col_tiles * TILE
    chips = cols // CORES
    most = most_steps(chips)
    square = rows == 4
    tall = height // PARTS
    swap = mates(cols)
    ring = list(range(0, cols, CORES)) + list(range(cols - 1, 0, -CORES))
    around = [(ring[i], ring[(i + 1) % cols]) for i in range(cols)]
    rows_start = 3 * most + SECTIONS

    def stack(slots):
        return jax.ShapeDtypeStruct((slots, TILE, width), BF16)

    def turn(array, bits):
        pairs = [(r * cols + c, (r ^ bits[c % CORES]) * cols + c) for r in range(rows) for c in range(cols)]
        return lax.ppermute(array, ("row", "col"), pairs)

    got = [lax.ppermute(piece, "col", swap) for piece in masked]
    if square:
        own_rows = pl.pallas_call(
            functools.partial(own_rows_kernel, col_tiles, row_tiles, rows_start),
            out_shape=(stack(PAIR),) * (in_row // PAIR),
            in_specs=[VMEM] * (1 + PARTS),
            out_specs=(VMEM,) * (in_row // PAIR),
            compiler_params=PARAMS,
            name="own_rows",
        )(table, *masked)
        got_rows = [turn(own, (1, 2)) for own in own_rows]
    else:
        own_rows = pl.pallas_call(
            functools.partial(masked_rows_kernel, col_tiles, row_tiles),
            out_shape=stack(SECTIONS),
            in_specs=[SMEM] + [VMEM] * PARTS,
            out_specs=VMEM,
            compiler_params=PARAMS,
            name="masked_rows",
        )(sections, *masked)
        right = lax.psum(own_rows, "row")

    direct, passed = [], []
    for t in range(steps):
        operands = [table, masked[t % PARTS], got[t % PARTS]]
        specs = [VMEM] * len(operands)
        if t >= LAG:
            operands.append(direct[t - LAG])
            specs.append(VMEM)
        order = [sent] if t > 0 else []
        if t >= LAG + 2:
            order.append(passed[t - LAG - (1 if t == steps - 1 and in_row == PAIR else 2)])
        if square and t == in_row + 1:
            order += got_rows
        operands += order
        specs += [ANY] * len(order)
        sent = pl.pallas_call(
            functools.partial(choose_kernel, col_tiles, t),
            out_shape=jax.ShapeDtypeStruct((tall, TILE), BF16),
            in_specs=specs,
            out_specs=VMEM,
            compiler_params=PARAMS,
            name="choose",
        )(*operands)
        if t >= LAG:
            sent, piece = lax.optimization_barrier((sent, direct[t - LAG]))
            passed.append(lax.ppermute(piece, "col", swap))
        direct.append(lax.ppermute(sent, "col", around))
    passed.append(lax.ppermute(direct[-2], "col", swap))

    if square:
        near = pl.pallas_call(
            functools.partial(near_rows_kernel, rows_start + SECTIONS),
            out_shape=stack(in_pair),
            in_specs=[VMEM] + [VMEM] * (2 * len(own_rows)) + [ANY],
            out_specs=VMEM,
            compiler_params=PARAMS,
            name="near_rows",
        )(table, *own_rows, *got_rows, direct[1 if in_row == PAIR else 2])
        right = pl.pallas_call(
            functools.partial(all_rows_kernel, rows_start + 2 * SECTIONS),
            out_shape=stack(SECTIONS),
            in_specs=[VMEM] * 3,
            out_specs=VMEM,
            compiler_params=PARAMS,
            name="all_rows",
        )(table, *lax.optimization_barrier((near, turn(near, (2, 1)), sent))[:2])
    right = right.reshape(SECTIONS * TILE, width)

    panel = jax.ShapeDtypeStruct((tall, SECTIONS * TILE), BF16)
    partial = jax.ShapeDtypeStruct((tall, width), jnp.float32)
    result = jax.ShapeDtypeStruct((height, width), BF16)
    buffers = [pltpu.VMEM((col_tiles, tall, TILE), BF16), pltpu.SemaphoreType.DMA((col_tiles, BLOCKS))]
    times = [list(range(part, steps - PARTS, PARTS)) for part in range(PARTS)]
    piece, right = lax.optimization_barrier((sent, right))
    operands = [array for part in range(PARTS) for array in (masked[part], got[part])]
    for part in range(PARTS):
        operands += [direct[t] for t in times[part]] + [passed[t] for t in times[part]]
    operands.append(piece)
    left = pl.pallas_call(
        functools.partial(gather_kernel, col_tiles, chips, times, steps),
        out_shape=(panel,) * PARTS,
        in_specs=[VMEM] * len(operands) + [ANY],
        out_specs=(VMEM,) * PARTS,
        compiler_params=PARAMS,
        name="gather",
    )(table, *operands)
    *left, right, direct[-2] = lax.optimization_barrier((*left, right, direct[-2]))
    early = pl.pallas_call(
        early_product_kernel,
        out_shape=(partial,) * PARTS,
        in_specs=[VMEM] * (PARTS + 1),
        out_specs=(VMEM,) * PARTS,
        compiler_params=PARAMS,
        name="early_product",
    )(*left, right)
    direct[-1], passed[-1], *early = lax.optimization_barrier((direct[-1], passed[-1], *early))
    passed.append(lax.ppermute(direct[-1], "col", swap))

    def add_last(t, before):
        return pl.pallas_call(
            functools.partial(add_last_kernel, most, t),
            out_shape=result,
            in_specs=[VMEM] * 5 + [HBM] * len(before),
            out_specs=HBM,
            input_output_aliases={5: 0} if before else {},
            scratch_shapes=buffers,
            compiler_params=PARAMS,
            name="add_last",
        )(table, early[t % PARTS], right, direct[t], passed[t], *before)

    return add_last(steps - 1, (add_last(steps - 2, ()),))


def shards(rows, cols, values, pattern, sections):
    row_tiles, col_tiles = pattern.shape
    height, width = values.shape
    chips = cols // CORES
    most = most_steps(chips)
    panel = jax.ShapeDtypeStruct((height // PARTS, width), BF16)
    *masked, table, which = pl.pallas_call(
        functools.partial(prepare_kernel, rows, col_tiles, row_tiles, chips),
        out_shape=(panel,) * PARTS
        + (
            jax.ShapeDtypeStruct((-(-table_rows(chips)[2] // 8) * 8, 128), jnp.int32),
            jax.ShapeDtypeStruct((1,), jnp.int32),
        ),
        in_specs=[HBM, HBM, HBM],
        out_specs=(VMEM,) * (PARTS + 1) + (SMEM,),
        scratch_shapes=[
            pltpu.SMEM(sections.shape, jnp.int32),
            pltpu.SMEM((col_tiles, row_tiles), jnp.int32),
            pltpu.SemaphoreType.DMA((row_tiles,)),
            pltpu.SemaphoreType.DMA((2,)),
        ],
        compiler_params=pltpu.CompilerParams(vmem_limit_bytes=62 * 1024 * 1024),
        name="prepare",
    )(sections, pattern.T, values)
    branches = [
        functools.partial(program, rows, cols, col_tiles, row_tiles, sizes) for sizes in size_keys(rows, chips)
    ]
    return lax.switch(which[0], branches, sections, table, *masked)


def solution(mesh):
    body = functools.partial(shards, mesh.shape["row"], mesh.shape["col"])
    in_specs = (P("row", "col"), P("row", "col"), P())
    return jax.shard_map(body, mesh=mesh, in_specs=in_specs, out_specs=P("row", "col"), check_vma=False)
```
